32 devices in a mesh: band: 2 (over x), grid: 16 (over z, y, core).
Axes of the slice: x: 2, y: 2, z: 4, core: 2. Of those that a mesh axis runs over, the one named last changes fastest.
Arguments:
- orbitals: float32 [64, 64, 12, 128], P('band', 'grid'), may hold values from -700 to 700
- potential: float32 [64, 12, 128], P('grid'), may hold values from 0.2 to 2
Outputs:
- basis: float32 [64, 64, 12, 128], P('band', 'grid')
The draws below stay inside these ranges and needn't reach their ends.
All inputs are finite; a program needn't handle non-finite values.
Results may differ from the reference program's by a relative error of at most 0.0001.
Values sent between devices are 32-bit elements; how exact they have to be, the bound alone decides.
A program may use at most 64 MiB of HBM per device.

```python
import math
import jax
import jax.numpy as jnp
from jax import lax

BANDS_DEV = 32
NY = 12
NZ = 128
NX = 64
BANDS = 64
N_BAND = 2


def draw_orbitals(key, part):
    key = jax.random.fold_in(key, 11)
    keys = jax.random.split(key, 3)
    band_scale = 10.0 ** jax.random.uniform(keys[0], (BANDS, 1, 1, 1), jnp.float32)
    cell_scale = 10.0 ** (0.5 * jax.random.uniform(keys[1], (1, NX, NY, NZ), jnp.float32))
    along = (jnp.arange(NX, dtype=jnp.float32) / NX).reshape(1, NX, 1, 1)
    values = jnp.clip(jax.random.normal(keys[2], (BANDS, NX, NY, NZ), jnp.float32), -5.0, 5.0)
    envelope = 10.0 ** (0.5 * along)
    return (values * band_scale * cell_scale * envelope).astype(jnp.float32)


def level_of(own_key, shape, cuts, low, high):
    def one(position, blocks):
        steps = jax.random.uniform(jax.random.fold_in(jax.random.fold_in(own_key, 6), position), (blocks,), jnp.float32, low / len(cuts), high / len(cuts))
        return jnp.repeat(jnp.exp(steps), shape[position] // blocks).reshape((-1,) + (1,) * (len(shape) - position - 1))

    gain = one(*cuts[0])
    for cut in cuts[1:]:
        gain = gain * one(*cut)
    return gain


def setup_inputs(seed: int = 0) -> dict:
    splits = jax.random.split(jax.random.key(seed), 3)
    return {
        "orbitals": draw_orbitals(jax.random.fold_in(splits[2], 71), 0),
        "potential": jnp.clip(jnp.exp(math.log(2.0) - 2.3025851 * jax.random.uniform(splits[1], (NX, NY, NZ), jnp.float32) ** level_of(splits[1], (NX, NY, NZ), ((0, 16),), -0.2, 0.2)), 0.2, 2.0),
    }


STENCIL = (-205.0 / 72.0, 8.0 / 5.0, -1.0 / 5.0, 8.0 / 315.0, -1.0 / 560.0)
MIDDLE = 6.875
SPREAD = 3.875

def apply_ham(field, potential):
    laplace = 3.0 * STENCIL[0] * field
    for m in range(1, 5):
        beside_all = jnp.roll(field, m, 1) + jnp.roll(field, -m, 1)
        beside_all = beside_all + jnp.roll(field, m, 2) + jnp.roll(field, -m, 2)
        beside_all = beside_all + jnp.roll(field, m, 3) + jnp.roll(field, -m, 3)
        laplace = laplace + STENCIL[m] * beside_all
    return -0.5 * laplace + potential[None] * field

def filter_group(field, potential):
    first_step = (apply_ham(field, potential) - MIDDLE * field) / SPREAD
    second = 2.0 * (apply_ham(first_step, potential) - MIDDLE * first_step) / SPREAD - field
    return second.reshape(field.shape[0], -1)

def reference(orbitals, potential):
    grouped = orbitals.reshape(N_BAND, BANDS_DEV, NX, NY, NZ)
    filtered = lax.map(lambda group: filter_group(group, potential), grouped)
    total_cells = NX * NY * NZ
    results = []
    for g in range(N_BAND):
        block = filtered[g]
        for earlier in results:
            coeffs = jnp.dot(earlier, block.T, precision=lax.Precision.HIGHEST) / total_cells
            block = block - jnp.dot(coeffs.T, earlier, precision=lax.Precision.HIGHEST)
        margin = jnp.dot(block, block.T, precision=lax.Precision.HIGHEST) / total_cells
        factor = jnp.linalg.cholesky(margin)
        results.append(lax.linalg.triangular_solve(factor, block, left_side=True, lower=True))
    return jnp.stack(results).reshape(BANDS, NX, NY, NZ)
```

```python
import functools

import jax
import jax.numpy as jnp
from jax import lax
from jax.experimental import pallas as pl
from jax.experimental.pallas import tpu as pltpu
from jax.sharding import PartitionSpec as P

STENCIL = (-205.0 / 72.0, 8.0 / 5.0, -1.0 / 5.0, 8.0 / 315.0, -1.0 / 560.0)
MIDDLE = 6.875
SPREAD = 3.875
ROWS = 8
MESH = pl.DeviceIdType.MESH


def padded_2(cells, sides, width):
    for axis, dim in sides:
        count = lax.axis_size(axis)
        head = lax.slice_in_dim(cells, 0, width, axis=dim)
        tail = lax.slice_in_dim(cells, cells.shape[dim] - width, cells.shape[dim], axis=dim)
        cells = jnp.concatenate(
            [
                lax.ppermute(tail, axis, [(i, (i + 1) % count) for i in range(count)]),
                cells,
                lax.ppermute(head, axis, [((i + 1) % count, i) for i in range(count)]),
            ],
            axis=dim,
        )
    return cells


def from_root(value, axis, source):
    kept = jnp.where(lax.axis_index(axis) == source, value, 0).astype(value.dtype)
    return lax.psum(kept, axis)


def apply_ham(field, potential):
    padded = padded_2(field, (("grid", 1),), 4)
    planes = field.shape[1]
    laplace = 3.0 * STENCIL[0] * field
    for m in range(1, 5):
        beside_all = padded[:, 4 + m : 4 + m + planes] + padded[:, 4 - m : 4 - m + planes]
        beside_all = beside_all + jnp.roll(field, m, 2) + jnp.roll(field, -m, 2)
        beside_all = beside_all + jnp.roll(field, m, 3) + jnp.roll(field, -m, 3)
        laplace = laplace + STENCIL[m] * beside_all
    return -0.5 * laplace + potential[None] * field


def products(left, right):
    return jnp.dot(left, right.T, precision=lax.Precision.HIGHEST)


def on_device_any(orbitals, potential):
    first_step = (apply_ham(orbitals, potential) - MIDDLE * orbitals) / SPREAD
    second = 2.0 * (apply_ham(first_step, potential) - MIDDLE * first_step) / SPREAD - orbitals
    group_rows = orbitals.shape[0]
    filtered = second.reshape(group_rows, -1)
    total_cells = filtered.shape[1] * lax.axis_size("grid")
    position = lax.axis_index("band")
    groups = lax.axis_size("band")
    result = jnp.zeros_like(filtered)
    residual_block = filtered
    margin = lax.psum(products(filtered, filtered), "grid") / total_cells
    for h in range(groups):
        factor = jnp.linalg.cholesky(margin)
        orthonormal = lax.linalg.triangular_solve(
            factor, residual_block, left_side=True, lower=True
        )
        result = jnp.where(position == h, orthonormal, result)
        if h + 1 < groups:
            finished = from_root(orthonormal, "band", h)
            coeffs = lax.psum(products(finished, residual_block), "grid") / total_cells
            pending = position > h
            residual_block = jnp.where(
                pending,
                residual_block - jnp.dot(coeffs.T, finished, precision=lax.Precision.HIGHEST),
                residual_block,
            )
            margin = jnp.where(
                pending, margin - jnp.dot(coeffs.T, coeffs, precision=lax.Precision.HIGHEST), margin
            )
    return result.reshape(orbitals.shape)


def chebyshev_step(ext, pot_ref, c, p):
    here = ext[c, 4 + p]
    ny = here.shape[0]
    pot = pot_ref[p].reshape(ny, 1, here.shape[2])
    out = here * ((pot - (MIDDLE + 1.5 * STENCIL[0])) / SPREAD)
    for m in range(1, 5):
        beside = ext[c, 4 + p + m] + ext[c, 4 + p - m]
        beside = beside + jnp.concatenate([here[ny - m :], here[: ny - m]], axis=0)
        beside = beside + jnp.concatenate([here[m:], here[:m]], axis=0)
        beside = beside + pltpu.roll(here, m, 2) + pltpu.roll(here, here.shape[2] - m, 2)
        out = out + (-0.5 * STENCIL[m] / SPREAD) * beside
    return out


def inverse_factor(gram):
    size = gram.shape[0]
    lanes = lax.broadcasted_iota(jnp.int32, (ROWS, 2 * size), 1)
    rows = lax.broadcasted_iota(jnp.int32, (ROWS, 2 * size), 0)
    unit_rows = lax.broadcasted_iota(jnp.int32, (size, size), 0)
    unit_lanes = lax.broadcasted_iota(jnp.int32, (size, size), 1)
    unit = jnp.where(unit_rows == unit_lanes, 1.0, 0.0).astype(jnp.float32)
    whole = jnp.concatenate([gram, unit], axis=1)
    blocks = [whole[ROWS * k : ROWS * (k + 1)] for k in range(size // ROWS)]
    for j in range(size):
        own, at = divmod(j, ROWS)
        row = blocks[own][at : at + 1]
        row = row / row[:, j : j + 1]
        for k in range(own, size // ROWS):
            less = blocks[k] - blocks[k][:, j : j + 1] * row
            blocks[k] = jnp.where(rows > at, less, blocks[k]) if k == own else less
    scaled = []
    for k, block in enumerate(blocks):
        pivot = jnp.sum(jnp.where(lanes == rows + ROWS * k, block, 0.0), axis=1, keepdims=True)
        scaled.append(block[:, size:] / jnp.sqrt(pivot))
    return jnp.concatenate(scaled, axis=0)


def split(value):
    high = value.astype(jnp.bfloat16)
    return high, (value - high.astype(jnp.float32)).astype(jnp.bfloat16)


def kernel(
    n, x_ref, pot_ref, out_ref,
    ext, ext2, fil, fil0, both, near, far,
    send1, recv1, send2, recv2, sendx, recvx, sendn, recvn, sendf, recvf,
):
    chunks, planes, ny = x_ref.shape[:3]
    lines = planes * ny
    me = lax.axis_index("grid")
    band = lax.axis_index("band")
    right, left = lax.rem(me + 1, n), lax.rem(me + n - 1, n)
    inner = 4
    outer = n // inner
    q, zz = lax.rem(me, inner), lax.div(me, inner)
    near_peers = [zz * inner + lax.rem(q + k, inner) for k in range(1, inner)]
    far_peers = [lax.rem(zz + k, outer) * inner + q for k in range(1, outer)]
    partner = {"band": 1 - band}

    barrier = pltpu.get_barrier_semaphore()
    peers = [{"grid": d} for d in [left, right] + near_peers + far_peers] + [partner]
    for peer in peers:
        pl.semaphore_signal(barrier, inc=1, device_id=peer, device_id_type=MESH)
    pl.semaphore_wait(barrier, len(peers))

    own = pl.ds(4, planes)

    def halo(src, dst, send, recv, c, side):
        where = pl.ds(0, 4) if side == 0 else pl.ds(4 + planes, 4)
        return pltpu.make_async_remote_copy(
            src_ref=src, dst_ref=dst.at[c, where],
            send_sem=send.at[side, c], recv_sem=recv.at[side, c],
            device_id={"grid": right if side == 0 else left}, device_id_type=MESH,
        )

    def halo1(c, side):
        return halo(x_ref.at[c], ext, send1, recv1, c, side)

    def halo2(c, side):
        return halo(ext2.at[c, own], ext2, send2, recv2, c, side)

    def across(c):
        return pltpu.make_async_remote_copy(
            src_ref=fil.at[c], dst_ref=fil0.at[c],
            send_sem=sendx.at[c], recv_sem=recvx.at[c],
            device_id=partner, device_id_type=MESH,
        )

    def begin(c, carry):
        halo1(c, 0).start()
        halo1(c, 1).start()
        ext[c, own] = x_ref[c]
        return carry

    lax.fori_loop(0, chunks, begin, 0)

    def first(c, carry):
        halo1(c, 0).wait_recv()
        halo1(c, 1).wait_recv()
        for p in range(planes):
            ext2[c, 4 + p] = chebyshev_step(ext, pot_ref, c, p)
        halo2(c, 0).start()
        halo2(c, 1).start()
        return carry

    lax.fori_loop(0, chunks, first, 0)

    def second(c, carry):
        halo2(c, 0).wait_recv()
        halo2(c, 1).wait_recv()
        for p in range(planes):
            value = 2.0 * chebyshev_step(ext2, pot_ref, c, p) - ext[c, 4 + p]
            fil[c, pl.ds(p * ny, ny)] = value

        @pl.when(band == 0)
        def _():
            across(c).start()
            fil0[c] = fil[c]

        return carry

    lax.fori_loop(0, chunks, second, 0)

    @pl.when(band == 1)
    def _():
        for c in range(chunks):
            across(c).wait_recv()

    rows = chunks * ROWS
    size = 2 * rows

    def pair(i):
        def at(ref, line):
            return ref[:, line].reshape(rows, ref.shape[3])

        return jnp.concatenate(
            [
                jnp.concatenate([at(fil0, 2 * i + t), at(fil, 2 * i + t)], axis=0)
                for t in range(2)
            ],
            axis=1,
        )

    def gram(i, total):
        high, low = split(pair(i))
        tall = jnp.concatenate([high, low], axis=0)
        both[i] = tall
        return total + lax.dot_general(
            tall, tall, (((1,), (1,)), ((), ())), preferred_element_type=jnp.float32
        )

    total = lax.fori_loop(0, lines // 2, gram, jnp.zeros((2 * size, 2 * size), jnp.float32))
    total = total[:size] + total[size:]
    total = total[:, :size] + total[:, size:]
    packed = jnp.concatenate([total[:rows], total[rows:]], axis=1)

    def exchange(value, slots, send, recv, place, peers, sources):
        slots[place] = value
        copies = [
            pltpu.make_async_remote_copy(
                src_ref=slots.at[place], dst_ref=slots.at[place],
                send_sem=send.at[k], recv_sem=recv.at[k],
                device_id={"grid": peer}, device_id_type=MESH,
            )
            for k, peer in enumerate(peers)
        ]
        for copy in copies:
            copy.start()
        for copy in copies:
            copy.wait_send()
        for k, source in enumerate(sources):
            pltpu.make_async_remote_copy(
                src_ref=slots.at[source], dst_ref=slots.at[source],
                send_sem=send.at[k], recv_sem=recv.at[k],
                device_id={"grid": peers[k]}, device_id_type=MESH,
            ).wait_recv()
        out = slots[0]
        for k in range(1, slots.shape[0]):
            out = out + slots[k]
        return out

    near_from = [lax.rem(q + inner - k, inner) for k in range(1, inner)]
    far_from = [lax.rem(zz + outer - k, outer) for k in range(1, outer)]
    packed = exchange(packed, near, sendn, recvn, q, near_peers, near_from)
    packed = exchange(packed, far, sendf, recvf, zz, far_peers, far_from)
    packed = packed / (lines * x_ref.shape[4] * n)
    inverse = inverse_factor(jnp.concatenate([packed[:, :size], packed[:, size:]], axis=0))
    weights = jnp.where(band == 0, inverse[:rows], inverse[rows:])
    high, low = split(weights)
    tall = jnp.concatenate([high, low], axis=0)
    wide = jnp.concatenate([tall, tall], axis=1)

    def final(i, carry):
        out = jnp.dot(wide, both[i], preferred_element_type=jnp.float32)
        out = out[:rows] + out[rows:]
        half = out.shape[1] // 2
        out_ref[2 * i] = out[:, :half]
        out_ref[2 * i + 1] = out[:, half:]
        return carry

    lax.fori_loop(0, lines // 2, final, 0)

    for c in range(chunks):
        for side in range(2):
            halo1(c, side).wait_send()
            halo2(c, side).wait_send()

    @pl.when(band == 0)
    def _():
        for c in range(chunks):
            across(c).wait_send()


def on_device_two(n, orbitals, potential):
    rows, planes, ny, nz = orbitals.shape
    chunks = rows // ROWS
    x = orbitals.reshape(chunks, ROWS, planes, ny, nz).transpose(0, 2, 3, 1, 4)
    f32, dma = jnp.float32, pltpu.SemaphoreType.DMA
    out = pl.pallas_call(
        functools.partial(kernel, n),
        out_shape=jax.ShapeDtypeStruct((planes * ny, rows, nz), f32),
        in_specs=[pl.BlockSpec(memory_space=pltpu.VMEM)] * 2,
        out_specs=pl.BlockSpec(memory_space=pltpu.VMEM),
        scratch_shapes=[
            pltpu.VMEM((chunks, planes + 8, ny, ROWS, nz), f32),
            pltpu.VMEM((chunks, planes + 8, ny, ROWS, nz), f32),
            pltpu.VMEM((chunks, planes * ny, ROWS, nz), f32),
            pltpu.VMEM((chunks, planes * ny, ROWS, nz), f32),
            pltpu.VMEM((planes * ny // 2, 4 * rows, 2 * nz), jnp.bfloat16),
            pltpu.VMEM((4, rows, 4 * rows), f32),
            pltpu.VMEM((n // 4, rows, 4 * rows), f32),
            dma((2, chunks)), dma((2, chunks)), dma((2, chunks)), dma((2, chunks)),
            dma((chunks,)), dma((chunks,)),
            dma((3,)), dma((3,)), dma((n // 4 - 1,)), dma((n // 4 - 1,)),
        ],
        compiler_params=pltpu.CompilerParams(
            collective_id=0, has_side_effects=True, vmem_limit_bytes=40 * 1024 * 1024
        ),
    )(x, potential)
    return out.reshape(planes, ny, rows, nz).transpose(2, 0, 1, 3)


def solution(mesh):
    n = mesh.shape["grid"]
    one_kernel = mesh.shape["band"] == 2 and n % 4 == 0 and n > 4
    on_device = functools.partial(on_device_two, n) if one_kernel else on_device_any
    in_specs = (P("band", "grid", None, None), P("grid", None, None))
    out_specs = P("band", "grid", None, None)
    return jax.shard_map(
        on_device, mesh=mesh, in_specs=in_specs, out_specs=out_specs, check_vma=False
    )
```

```python
import functools

import jax
import jax.numpy as jnp
from jax import lax
from jax.experimental import pallas as pl
from jax.experimental.pallas import tpu as pltpu
from jax.sharding import PartitionSpec as P

STENCIL = (-205.0 / 72.0, 8.0 / 5.0, -1.0 / 5.0, 8.0 / 315.0, -1.0 / 560.0)
MIDDLE = 6.875
SPREAD = 3.875
ROWS = 8
UNROLL = 12
MESH = pl.DeviceIdType.MESH


def padded_2(cells, sides, width):
    for axis, dim in sides:
        count = lax.axis_size(axis)
        head = lax.slice_in_dim(cells, 0, width, axis=dim)
        tail = lax.slice_in_dim(cells, cells.shape[dim] - width, cells.shape[dim], axis=dim)
        cells = jnp.concatenate(
            [
                lax.ppermute(tail, axis, [(i, (i + 1) % count) for i in range(count)]),
                cells,
                lax.ppermute(head, axis, [((i + 1) % count, i) for i in range(count)]),
            ],
            axis=dim,
        )
    return cells


def from_root(value, axis, source):
    kept = jnp.where(lax.axis_index(axis) == source, value, 0).astype(value.dtype)
    return lax.psum(kept, axis)


def apply_ham(field, potential):
    padded = padded_2(field, (("grid", 1),), 4)
    planes = field.shape[1]
    laplace = 3.0 * STENCIL[0] * field
    for m in range(1, 5):
        beside_all = padded[:, 4 + m : 4 + m + planes] + padded[:, 4 - m : 4 - m + planes]
        beside_all = beside_all + jnp.roll(field, m, 2) + jnp.roll(field, -m, 2)
        beside_all = beside_all + jnp.roll(field, m, 3) + jnp.roll(field, -m, 3)
        laplace = laplace + STENCIL[m] * beside_all
    return -0.5 * laplace + potential[None] * field


def products(left, right):
    return jnp.dot(left, right.T, precision=lax.Precision.HIGHEST)


def on_device_any(orbitals, potential):
    first_step = (apply_ham(orbitals, potential) - MIDDLE * orbitals) / SPREAD
    second = 2.0 * (apply_ham(first_step, potential) - MIDDLE * first_step) / SPREAD - orbitals
    group_rows = orbitals.shape[0]
    filtered = second.reshape(group_rows, -1)
    total_cells = filtered.shape[1] * lax.axis_size("grid")
    position = lax.axis_index("band")
    groups = lax.axis_size("band")
    result = jnp.zeros_like(filtered)
    residual_block = filtered
    margin = lax.psum(products(filtered, filtered), "grid") / total_cells
    for h in range(groups):
        factor = jnp.linalg.cholesky(margin)
        orthonormal = lax.linalg.triangular_solve(
            factor, residual_block, left_side=True, lower=True
        )
        result = jnp.where(position == h, orthonormal, result)
        if h + 1 < groups:
            finished = from_root(orthonormal, "band", h)
            coeffs = lax.psum(products(finished, residual_block), "grid") / total_cells
            pending = position > h
            residual_block = jnp.where(
                pending,
                residual_block - jnp.dot(coeffs.T, finished, precision=lax.Precision.HIGHEST),
                residual_block,
            )
            margin = jnp.where(
                pending, margin - jnp.dot(coeffs.T, coeffs, precision=lax.Precision.HIGHEST), margin
            )
    return result.reshape(orbitals.shape)


def chebyshev_step(ext, pot_ref, c, p):
    here = ext[c, 4 + p]
    ny = here.shape[0]
    pot = pot_ref[:, p : p + 1, :]
    out = here * ((pot - (MIDDLE + 1.5 * STENCIL[0])) / SPREAD)
    for m in range(1, 5):
        beside = ext[c, 4 + p + m] + ext[c, 4 + p - m]
        beside = beside + jnp.concatenate([here[ny - m :], here[: ny - m]], axis=0)
        beside = beside + jnp.concatenate([here[m:], here[:m]], axis=0)
        beside = beside + pltpu.roll(here, m, 2) + pltpu.roll(here, here.shape[2] - m, 2)
        out = out + (-0.5 * STENCIL[m] / SPREAD) * beside
    return out


def inverse_factor(gram):
    size = gram.shape[0]
    lanes = lax.broadcasted_iota(jnp.int32, (ROWS, 2 * size), 1)
    rows = lax.broadcasted_iota(jnp.int32, (ROWS, 2 * size), 0)
    unit_rows = lax.broadcasted_iota(jnp.int32, (size, size), 0)
    unit_lanes = lax.broadcasted_iota(jnp.int32, (size, size), 1)
    unit = jnp.where(unit_rows == unit_lanes, 1.0, 0.0).astype(jnp.float32)
    whole = jnp.concatenate([gram, unit], axis=1)
    blocks = [whole[ROWS * k : ROWS * (k + 1)] for k in range(size // ROWS)]
    for j in range(0, size, 2):
        own, at = divmod(j, ROWS)
        row0, row1 = blocks[own][at : at + 1], blocks[own][at + 1 : at + 2]
        scale = 1.0 / row0[:, j : j + 1]
        across = row0[:, j + 1 : j + 2]
        ratio = row1[:, j : j + 1] * scale
        row1_left = row1 - ratio * row0
        cross = across * scale
        unit0 = row0 * scale
        unit1 = row1_left / (row1[:, j + 1 : j + 2] - ratio * across)
        for k in range(own, size // ROWS):
            col0 = blocks[k][:, j : j + 1]
            col1 = blocks[k][:, j + 1 : j + 2] - col0 * cross
            less = blocks[k] - col0 * unit0 - col1 * unit1
            if k == own:
                less = jnp.where(rows > at + 1, less, blocks[k])
                less = jnp.where(rows == at + 1, row1_left, less)
            blocks[k] = less
    scaled = []
    for k, block in enumerate(blocks):
        pivot = jnp.sum(jnp.where(lanes == rows + ROWS * k, block, 0.0), axis=1, keepdims=True)
        scaled.append(block[:, size:] / jnp.sqrt(pivot))
    return jnp.concatenate(scaled, axis=0)


def split(value):
    high = value.astype(jnp.bfloat16)
    return high, (value - high.astype(jnp.float32)).astype(jnp.bfloat16)


def kernel(
    n, x_ref, pot_ref, out_ref,
    ext, ext2, fil, fil0, both, near, far,
    send1, recv1, send2, recv2, sendx, recvx, sendn, recvn, sendf, recvf,
):
    chunks, planes, ny = x_ref.shape[:3]
    lines = planes * ny
    me = lax.axis_index("grid")
    band = lax.axis_index("band")
    right, left = lax.rem(me + 1, n), lax.rem(me + n - 1, n)
    inner = 4
    outer = n // inner
    q, zz = lax.rem(me, inner), lax.div(me, inner)
    near_peers = [zz * inner + lax.rem(q + k, inner) for k in range(1, inner)]
    far_peers = [lax.rem(zz + k, outer) * inner + q for k in range(1, outer)]
    partner = {"band": 1 - band}

    barrier = pltpu.get_barrier_semaphore()
    peers = [{"grid": d} for d in [left, right] + near_peers + far_peers] + [partner]
    for peer in peers:
        pl.semaphore_signal(barrier, inc=1, device_id=peer, device_id_type=MESH)
    pl.semaphore_wait(barrier, len(peers))

    own = pl.ds(4, planes)

    def halo(src, dst, send, recv, c, side):
        where = pl.ds(0, 4) if side == 0 else pl.ds(4 + planes, 4)
        return pltpu.make_async_remote_copy(
            src_ref=src, dst_ref=dst.at[c, where],
            send_sem=send.at[side, c], recv_sem=recv.at[side, c],
            device_id={"grid": right if side == 0 else left}, device_id_type=MESH,
        )

    def halo1(c, side):
        return halo(x_ref.at[c], ext, send1, recv1, c, side)

    def halo2(c, side):
        return halo(ext2.at[c, own], ext2, send2, recv2, c, side)

    def across(c):
        return pltpu.make_async_remote_copy(
            src_ref=fil.at[c], dst_ref=fil0.at[c],
            send_sem=sendx.at[c], recv_sem=recvx.at[c],
            device_id=partner, device_id_type=MESH,
        )

    def begin(c, carry):
        halo1(c, 0).start()
        halo1(c, 1).start()
        ext[c, own] = x_ref[c]
        return carry

    lax.fori_loop(0, chunks, begin, 0)

    def first(c, carry):
        halo1(c, 0).wait_recv()
        halo1(c, 1).wait_recv()
        for p in range(planes):
            ext2[c, 4 + p] = chebyshev_step(ext, pot_ref, c, p)
        halo2(c, 0).start()
        halo2(c, 1).start()
        return carry

    lax.fori_loop(0, chunks, first, 0)

    def second(c, carry):
        halo2(c, 0).wait_recv()
        halo2(c, 1).wait_recv()
        for p in range(planes):
            value = 2.0 * chebyshev_step(ext2, pot_ref, c, p) - ext[c, 4 + p]
            fil[c, pl.ds(p * ny, ny)] = value

        @pl.when(band == 0)
        def _():
            across(c).start()
            fil0[c] = fil[c]

        return carry

    lax.fori_loop(0, chunks, second, 0)

    @pl.when(band == 1)
    def _():
        for c in range(chunks):
            across(c).wait_recv()

    rows = chunks * ROWS
    size = 2 * rows

    def pair(i):
        def at(ref, line):
            return ref[:, line].reshape(rows, ref.shape[3])

        return jnp.concatenate(
            [
                jnp.concatenate([at(fil0, 2 * i + t), at(fil, 2 * i + t)], axis=0)
                for t in range(2)
            ],
            axis=1,
        )

    def gram(i, total):
        high, low = split(pair(i))
        tall = jnp.concatenate([high, low], axis=0)
        both[i] = tall
        return total + lax.dot_general(
            tall, tall, (((1,), (1,)), ((), ())), preferred_element_type=jnp.float32
        )

    total = lax.fori_loop(
        0, lines // 2, gram, jnp.zeros((2 * size, 2 * size), jnp.float32), unroll=UNROLL
    )
    total = total[:size] + total[size:]
    total = total[:, :size] + total[:, size:]
    packed = jnp.concatenate([total[:rows], total[rows:]], axis=1)

    def exchange(value, slots, send, recv, place, peers, sources):
        slots[place] = value
        copies = [
            pltpu.make_async_remote_copy(
                src_ref=slots.at[place], dst_ref=slots.at[place],
                send_sem=send.at[k], recv_sem=recv.at[k],
                device_id={"grid": peer}, device_id_type=MESH,
            )
            for k, peer in enumerate(peers)
        ]
        for copy in copies:
            copy.start()
        for copy in copies:
            copy.wait_send()
        for k, source in enumerate(sources):
            pltpu.make_async_remote_copy(
                src_ref=slots.at[source], dst_ref=slots.at[source],
                send_sem=send.at[k], recv_sem=recv.at[k],
                device_id={"grid": peers[k]}, device_id_type=MESH,
            ).wait_recv()
        out = slots[0]
        for k in range(1, slots.shape[0]):
            out = out + slots[k]
        return out

    near_from = [lax.rem(q + inner - k, inner) for k in range(1, inner)]
    far_from = [lax.rem(zz + outer - k, outer) for k in range(1, outer)]
    packed = exchange(packed, near, sendn, recvn, q, near_peers, near_from)
    packed = exchange(packed, far, sendf, recvf, zz, far_peers, far_from)
    packed = packed / (lines * x_ref.shape[4] * n)
    inverse = inverse_factor(jnp.concatenate([packed[:, :size], packed[:, size:]], axis=0))
    weights = jnp.where(band == 0, inverse[:rows], inverse[rows:])
    high, low = split(weights)
    tall = jnp.concatenate([high, low], axis=0)
    wide = jnp.concatenate([tall, tall], axis=1)

    def final(i, carry):
        out = jnp.dot(wide, both[i], preferred_element_type=jnp.float32)
        out = out[:rows] + out[rows:]
        half = out.shape[1] // 2
        out_ref[2 * i] = out[:, :half]
        out_ref[2 * i + 1] = out[:, half:]
        return carry

    lax.fori_loop(0, lines // 2, final, 0, unroll=UNROLL)

    for c in range(chunks):
        for side in range(2):
            halo1(c, side).wait_send()
            halo2(c, side).wait_send()

    @pl.when(band == 0)
    def _():
        for c in range(chunks):
            across(c).wait_send()


def on_device_two(n, orbitals, potential):
    rows, planes, ny, nz = orbitals.shape
    chunks = rows // ROWS
    x = orbitals.reshape(chunks, ROWS, planes, ny, nz).transpose(0, 2, 3, 1, 4)
    f32, dma = jnp.float32, pltpu.SemaphoreType.DMA
    out = pl.pallas_call(
        functools.partial(kernel, n),
        out_shape=jax.ShapeDtypeStruct((planes * ny, rows, nz), f32),
        in_specs=[pl.BlockSpec(memory_space=pltpu.VMEM)] * 2,
        out_specs=pl.BlockSpec(memory_space=pltpu.VMEM),
        scratch_shapes=[
            pltpu.VMEM((chunks, planes + 8, ny, ROWS, nz), f32),
            pltpu.VMEM((chunks, planes + 8, ny, ROWS, nz), f32),
            pltpu.VMEM((chunks, planes * ny, ROWS, nz), f32),
            pltpu.VMEM((chunks, planes * ny, ROWS, nz), f32),
            pltpu.VMEM((planes * ny // 2, 4 * rows, 2 * nz), jnp.bfloat16),
            pltpu.VMEM((4, rows, 4 * rows), f32),
            pltpu.VMEM((n // 4, rows, 4 * rows), f32),
            dma((2, chunks)), dma((2, chunks)), dma((2, chunks)), dma((2, chunks)),
            dma((chunks,)), dma((chunks,)),
            dma((3,)), dma((3,)), dma((n // 4 - 1,)), dma((n // 4 - 1,)),
        ],
        compiler_params=pltpu.CompilerParams(
            collective_id=0, has_side_effects=True, vmem_limit_bytes=40 * 1024 * 1024
        ),
    )(x, potential.transpose(1, 0, 2))
    return out.reshape(planes, ny, rows, nz).transpose(2, 0, 1, 3)


def solution(mesh):
    n = mesh.shape["grid"]
    one_kernel = mesh.shape["band"] == 2 and n % 4 == 0 and n > 4
    on_device = functools.partial(on_device_two, n) if one_kernel else on_device_any
    in_specs = (P("band", "grid", None, None), P("grid", None, None))
    out_specs = P("band", "grid", None, None)
    return jax.shard_map(
        on_device, mesh=mesh, in_specs=in_specs, out_specs=out_specs, check_vma=False
    )
```

```python
import functools

import jax
import jax.numpy as jnp
from jax import lax
from jax.experimental import pallas as pl
from jax.experimental.pallas import tpu as pltpu
from jax.sharding import PartitionSpec as P

STENCIL = (-205.0 / 72.0, 8.0 / 5.0, -1.0 / 5.0, 8.0 / 315.0, -1.0 / 560.0)
MIDDLE = 6.875
SPREAD = 3.875
ROWS = 8
UNROLL = 12
MESH = pl.DeviceIdType.MESH


def padded_2(cells, sides, width):
    for axis, dim in sides:
        count = lax.axis_size(axis)
        head = lax.slice_in_dim(cells, 0, width, axis=dim)
        tail = lax.slice_in_dim(cells, cells.shape[dim] - width, cells.shape[dim], axis=dim)
        cells = jnp.concatenate(
            [
                lax.ppermute(tail, axis, [(i, (i + 1) % count) for i in range(count)]),
                cells,
                lax.ppermute(head, axis, [((i + 1) % count, i) for i in range(count)]),
            ],
            axis=dim,
        )
    return cells


def from_root(value, axis, source):
    kept = jnp.where(lax.axis_index(axis) == source, value, 0).astype(value.dtype)
    return lax.psum(kept, axis)


def apply_ham(field, potential):
    padded = padded_2(field, (("grid", 1),), 4)
    planes = field.shape[1]
    laplace = 3.0 * STENCIL[0] * field
    for m in range(1, 5):
        beside_all = padded[:, 4 + m : 4 + m + planes] + padded[:, 4 - m : 4 - m + planes]
        beside_all = beside_all + jnp.roll(field, m, 2) + jnp.roll(field, -m, 2)
        beside_all = beside_all + jnp.roll(field, m, 3) + jnp.roll(field, -m, 3)
        laplace = laplace + STENCIL[m] * beside_all
    return -0.5 * laplace + potential[None] * field


def products(left, right):
    return jnp.dot(left, right.T, precision=lax.Precision.HIGHEST)


def on_device_any(orbitals, potential):
    first_step = (apply_ham(orbitals, potential) - MIDDLE * orbitals) / SPREAD
    second = 2.0 * (apply_ham(first_step, potential) - MIDDLE * first_step) / SPREAD - orbitals
    group_rows = orbitals.shape[0]
    filtered = second.reshape(group_rows, -1)
    total_cells = filtered.shape[1] * lax.axis_size("grid")
    position = lax.axis_index("band")
    groups = lax.axis_size("band")
    result = jnp.zeros_like(filtered)
    residual_block = filtered
    margin = lax.psum(products(filtered, filtered), "grid") / total_cells
    for h in range(groups):
        factor = jnp.linalg.cholesky(margin)
        orthonormal = lax.linalg.triangular_solve(
            factor, residual_block, left_side=True, lower=True
        )
        result = jnp.where(position == h, orthonormal, result)
        if h + 1 < groups:
            finished = from_root(orthonormal, "band", h)
            coeffs = lax.psum(products(finished, residual_block), "grid") / total_cells
            pending = position > h
            residual_block = jnp.where(
                pending,
                residual_block - jnp.dot(coeffs.T, finished, precision=lax.Precision.HIGHEST),
                residual_block,
            )
            margin = jnp.where(
                pending, margin - jnp.dot(coeffs.T, coeffs, precision=lax.Precision.HIGHEST), margin
            )
    return result.reshape(orbitals.shape)


def chebyshev_step(ext, pot_ref, c, p):
    here = ext[c, 4 + p]
    ny = here.shape[0]
    pot = pot_ref[:, p : p + 1, :]
    out = here * ((pot - (MIDDLE + 1.5 * STENCIL[0])) / SPREAD)
    for m in range(1, 5):
        beside = ext[c, 4 + p + m] + ext[c, 4 + p - m]
        beside = beside + jnp.concatenate([here[ny - m :], here[: ny - m]], axis=0)
        beside = beside + jnp.concatenate([here[m:], here[:m]], axis=0)
        beside = beside + pltpu.roll(here, m, 2) + pltpu.roll(here, here.shape[2] - m, 2)
        out = out + (-0.5 * STENCIL[m] / SPREAD) * beside
    return out


def inverse_factor(gram):
    size = gram.shape[0]
    lanes = lax.broadcasted_iota(jnp.int32, (ROWS, 2 * size), 1)
    rows = lax.broadcasted_iota(jnp.int32, (ROWS, 2 * size), 0)
    unit_rows = lax.broadcasted_iota(jnp.int32, (size, size), 0)
    unit_lanes = lax.broadcasted_iota(jnp.int32, (size, size), 1)
    unit = jnp.where(unit_rows == unit_lanes, 1.0, 0.0).astype(jnp.float32)
    whole = jnp.concatenate([gram, unit], axis=1)
    blocks = [whole[ROWS * k : ROWS * (k + 1)] for k in range(size // ROWS)]
    for j in range(0, size, 2):
        own, at = divmod(j, ROWS)
        row0, row1 = blocks[own][at : at + 1], blocks[own][at + 1 : at + 2]
        scale = 1.0 / row0[:, j : j + 1]
        across = row0[:, j + 1 : j + 2]
        ratio = row1[:, j : j + 1] * scale
        row1_left = row1 - ratio * row0
        cross = across * scale
        unit0 = row0 * scale
        unit1 = row1_left / (row1[:, j + 1 : j + 2] - ratio * across)
        for k in range(own, size // ROWS):
            col0 = blocks[k][:, j : j + 1]
            col1 = blocks[k][:, j + 1 : j + 2] - col0 * cross
            less = blocks[k] - col0 * unit0 - col1 * unit1
            if k == own:
                less = jnp.where(rows > at + 1, less, blocks[k])
                less = jnp.where(rows == at + 1, row1_left, less)
            blocks[k] = less
    scaled = []
    for k, block in enumerate(blocks):
        pivot = jnp.sum(jnp.where(lanes == rows + ROWS * k, block, 0.0), axis=1, keepdims=True)
        scaled.append(block[:, size:] / jnp.sqrt(pivot))
    return jnp.concatenate(scaled, axis=0)


def split(value):
    high = value.astype(jnp.bfloat16)
    return high, (value - high.astype(jnp.float32)).astype(jnp.bfloat16)


def kernel(
    n, x_ref, pot_ref, out_ref,
    ext, ext2, fil, fil0, both, near, far,
    send1, recv1, send2, recv2, sendx, recvx, sendn, recvn, sendf, recvf,
):
    chunks, planes, ny = x_ref.shape[:3]
    lines = planes * ny
    me = lax.axis_index("grid")
    band = lax.axis_index("band")
    right, left = lax.rem(me + 1, n), lax.rem(me + n - 1, n)
    inner = 4
    outer = n // inner
    q, zz = lax.rem(me, inner), lax.div(me, inner)
    near_peers = [zz * inner + lax.rem(q + k, inner) for k in range(1, inner)]
    far_peers = [lax.rem(zz + k, outer) * inner + q for k in range(1, outer)]
    partner = {"band": 1 - band}

    barrier = pltpu.get_barrier_semaphore()
    peers = [{"grid": d} for d in [left, right] + near_peers + far_peers] + [partner]
    for peer in peers:
        pl.semaphore_signal(barrier, inc=1, device_id=peer, device_id_type=MESH)
    pl.semaphore_wait(barrier, len(peers))

    own = pl.ds(4, planes)

    def halo(src, dst, send, recv, c, side):
        where = pl.ds(0, 4) if side == 0 else pl.ds(4 + planes, 4)
        return pltpu.make_async_remote_copy(
            src_ref=src, dst_ref=dst.at[c, where],
            send_sem=send.at[side, c], recv_sem=recv.at[side, c],
            device_id={"grid": right if side == 0 else left}, device_id_type=MESH,
        )

    def halo1(c, side):
        return halo(x_ref.at[c], ext, send1, recv1, c, side)

    def halo2(c, side):
        return halo(ext2.at[c, own], ext2, send2, recv2, c, side)

    def across(c, p):
        return pltpu.make_async_remote_copy(
            src_ref=fil.at[c, pl.ds(p * ny, ny)], dst_ref=fil0.at[c, pl.ds(p * ny, ny)],
            send_sem=sendx.at[c, p], recv_sem=recvx.at[c, p],
            device_id=partner, device_id_type=MESH,
        )

    def begin(c, carry):
        halo1(c, 0).start()
        halo1(c, 1).start()
        ext[c, own] = x_ref[c]
        return carry

    lax.fori_loop(0, chunks, begin, 0)

    def first(c, carry):
        halo1(c, 0).wait_recv()
        halo1(c, 1).wait_recv()
        for p in range(planes):
            ext2[c, 4 + p] = chebyshev_step(ext, pot_ref, c, p)
        halo2(c, 0).start()
        halo2(c, 1).start()
        return carry

    lax.fori_loop(0, chunks, first, 0)

    def second(c, carry):
        halo2(c, 0).wait_recv()
        halo2(c, 1).wait_recv()
        for p in range(planes):
            value = 2.0 * chebyshev_step(ext2, pot_ref, c, p) - ext[c, 4 + p]
            fil[c, pl.ds(p * ny, ny)] = value
            send_across(c, p)

        @pl.when(band == 0)
        def _():
            fil0[c] = fil[c]

        return carry

    def send_across(c, p):
        @pl.when(band == 0)
        def _():
            across(c, p).start()

    lax.fori_loop(0, chunks, second, 0)

    rows = chunks * ROWS
    size = 2 * rows

    def cast(ref, low_chunk, high_chunk, start):
        count = (high_chunk - low_chunk) * ROWS

        def one(i, carry):
            value = jnp.concatenate(
                [
                    ref[low_chunk:high_chunk, 2 * i + t].reshape(count, ref.shape[3])
                    for t in range(2)
                ],
                axis=1,
            )
            high, low = split(value)
            both[i, start : start + count] = high
            both[i, size + start : size + start + count] = low
            return carry

        lax.fori_loop(0, lines // 2, one, 0, unroll=4)

    def arrived(low_chunk, high_chunk):
        @pl.when(band == 1)
        def _():
            for c in range(low_chunk, high_chunk):
                for p in range(planes):
                    across(c, p).wait_recv()

    half_way = chunks // 2
    cast(fil, 0, chunks, rows)
    arrived(0, half_way)
    cast(fil0, 0, half_way, 0)
    arrived(half_way, chunks)
    cast(fil0, half_way, chunks, half_way * ROWS)

    def gram(i, total):
        tall = both[i]
        return total + lax.dot_general(
            tall, tall, (((1,), (1,)), ((), ())), preferred_element_type=jnp.float32
        )

    total = lax.fori_loop(
        0, lines // 2, gram, jnp.zeros((2 * size, 2 * size), jnp.float32), unroll=UNROLL
    )
    total = total[:size] + total[size:]
    total = total[:, :size] + total[:, size:]
    packed = jnp.concatenate([total[:rows], total[rows:]], axis=1)

    sent = []

    def exchange(value, slots, send, recv, place, peers, sources):
        slots[place] = value
        copies = [
            pltpu.make_async_remote_copy(
                src_ref=slots.at[place], dst_ref=slots.at[place],
                send_sem=send.at[k], recv_sem=recv.at[k],
                device_id={"grid": peer}, device_id_type=MESH,
            )
            for k, peer in enumerate(peers)
        ]
        for copy in copies:
            copy.start()
        for k, source in enumerate(sources):
            pltpu.make_async_remote_copy(
                src_ref=slots.at[source], dst_ref=slots.at[source],
                send_sem=send.at[k], recv_sem=recv.at[k],
                device_id={"grid": peers[k]}, device_id_type=MESH,
            ).wait_recv()
        sent.extend(copies)
        out = slots[0]
        for k in range(1, slots.shape[0]):
            out = out + slots[k]
        return out

    near_from = [lax.rem(q + inner - k, inner) for k in range(1, inner)]
    far_from = [lax.rem(zz + outer - k, outer) for k in range(1, outer)]
    packed = exchange(packed, near, sendn, recvn, q, near_peers, near_from)
    packed = exchange(packed, far, sendf, recvf, zz, far_peers, far_from)
    packed = packed / (lines * x_ref.shape[4] * n)
    inverse = inverse_factor(jnp.concatenate([packed[:, :size], packed[:, size:]], axis=0))
    weights = jnp.where(band == 0, inverse[:rows], inverse[rows:])
    high, low = split(weights)
    tall = jnp.concatenate([high, low], axis=0)
    wide = jnp.concatenate([tall, tall], axis=1)

    def final(i, carry):
        out = jnp.dot(wide, both[i], preferred_element_type=jnp.float32)
        out = out[:rows] + out[rows:]
        half = out.shape[1] // 2
        out_ref[2 * i] = out[:, :half]
        out_ref[2 * i + 1] = out[:, half:]
        return carry

    lax.fori_loop(0, lines // 2, final, 0, unroll=UNROLL)

    for copy in sent:
        copy.wait_send()
    for c in range(chunks):
        for side in range(2):
            halo1(c, side).wait_send()
            halo2(c, side).wait_send()

    @pl.when(band == 0)
    def _():
        for c in range(chunks):
            for p in range(planes):
                across(c, p).wait_send()


def on_device_two(n, orbitals, potential):
    rows, planes, ny, nz = orbitals.shape
    chunks = rows // ROWS
    x = orbitals.reshape(chunks, ROWS, planes, ny, nz).transpose(0, 2, 3, 1, 4)
    f32, dma = jnp.float32, pltpu.SemaphoreType.DMA
    out = pl.pallas_call(
        functools.partial(kernel, n),
        out_shape=jax.ShapeDtypeStruct((planes * ny, rows, nz), f32),
        in_specs=[pl.BlockSpec(memory_space=pltpu.VMEM)] * 2,
        out_specs=pl.BlockSpec(memory_space=pltpu.VMEM),
        scratch_shapes=[
            pltpu.VMEM((chunks, planes + 8, ny, ROWS, nz), f32),
            pltpu.VMEM((chunks, planes + 8, ny, ROWS, nz), f32),
            pltpu.VMEM((chunks, planes * ny, ROWS, nz), f32),
            pltpu.VMEM((chunks, planes * ny, ROWS, nz), f32),
            pltpu.VMEM((planes * ny // 2, 4 * rows, 2 * nz), jnp.bfloat16),
            pltpu.VMEM((4, rows, 4 * rows), f32),
            pltpu.VMEM((n // 4, rows, 4 * rows), f32),
            dma((2, chunks)), dma((2, chunks)), dma((2, chunks)), dma((2, chunks)),
            dma((chunks, planes)), dma((chunks, planes)),
            dma((3,)), dma((3,)), dma((n // 4 - 1,)), dma((n // 4 - 1,)),
        ],
        compiler_params=pltpu.CompilerParams(
            collective_id=0, has_side_effects=True, vmem_limit_bytes=40 * 1024 * 1024
        ),
    )(x, potential.transpose(1, 0, 2))
    return out.reshape(planes, ny, rows, nz).transpose(2, 0, 1, 3)


def solution(mesh):
    n = mesh.shape["grid"]
    one_kernel = mesh.shape["band"] == 2 and n % 4 == 0 and n > 4
    on_device = functools.partial(on_device_two, n) if one_kernel else on_device_any
    in_specs = (P("band", "grid", None, None), P("grid", None, None))
    out_specs = P("band", "grid", None, None)
    return jax.shard_map(
        on_device, mesh=mesh, in_specs=in_specs, out_specs=out_specs, check_vma=False
    )
```

```python
import functools

import jax
import jax.numpy as jnp
from jax import lax
from jax.experimental import pallas as pl
from jax.experimental.pallas import tpu as pltpu
from jax.sharding import PartitionSpec as P

STENCIL = (-205.0 / 72.0, 8.0 / 5.0, -1.0 / 5.0, 8.0 / 315.0, -1.0 / 560.0)
MIDDLE = 6.875
SPREAD = 3.875
ROWS = 8
UNROLL = 12
MESH = pl.DeviceIdType.MESH


def padded_2(cells, sides, width):
    for axis, dim in sides:
        count = lax.axis_size(axis)
        head = lax.slice_in_dim(cells, 0, width, axis=dim)
        tail = lax.slice_in_dim(cells, cells.shape[dim] - width, cells.shape[dim], axis=dim)
        cells = jnp.concatenate(
            [
                lax.ppermute(tail, axis, [(i, (i + 1) % count) for i in range(count)]),
                cells,
                lax.ppermute(head, axis, [((i + 1) % count, i) for i in range(count)]),
            ],
            axis=dim,
        )
    return cells


def from_root(value, axis, source):
    kept = jnp.where(lax.axis_index(axis) == source, value, 0).astype(value.dtype)
    return lax.psum(kept, axis)


def apply_ham(field, potential):
    padded = padded_2(field, (("grid", 1),), 4)
    planes = field.shape[1]
    laplace = 3.0 * STENCIL[0] * field
    for m in range(1, 5):
        beside_all = padded[:, 4 + m : 4 + m + planes] + padded[:, 4 - m : 4 - m + planes]
        beside_all = beside_all + jnp.roll(field, m, 2) + jnp.roll(field, -m, 2)
        beside_all = beside_all + jnp.roll(field, m, 3) + jnp.roll(field, -m, 3)
        laplace = laplace + STENCIL[m] * beside_all
    return -0.5 * laplace + potential[None] * field


def products(left, right):
    return jnp.dot(left, right.T, precision=lax.Precision.HIGHEST)


def on_device_any(orbitals, potential):
    first_step = (apply_ham(orbitals, potential) - MIDDLE * orbitals) / SPREAD
    second = 2.0 * (apply_ham(first_step, potential) - MIDDLE * first_step) / SPREAD - orbitals
    group_rows = orbitals.shape[0]
    filtered = second.reshape(group_rows, -1)
    total_cells = filtered.shape[1] * lax.axis_size("grid")
    position = lax.axis_index("band")
    groups = lax.axis_size("band")
    result = jnp.zeros_like(filtered)
    residual_block = filtered
    margin = lax.psum(products(filtered, filtered), "grid") / total_cells
    for h in range(groups):
        factor = jnp.linalg.cholesky(margin)
        orthonormal = lax.linalg.triangular_solve(
            factor, residual_block, left_side=True, lower=True
        )
        result = jnp.where(position == h, orthonormal, result)
        if h + 1 < groups:
            finished = from_root(orthonormal, "band", h)
            coeffs = lax.psum(products(finished, residual_block), "grid") / total_cells
            pending = position > h
            residual_block = jnp.where(
                pending,
                residual_block - jnp.dot(coeffs.T, finished, precision=lax.Precision.HIGHEST),
                residual_block,
            )
            margin = jnp.where(
                pending, margin - jnp.dot(coeffs.T, coeffs, precision=lax.Precision.HIGHEST), margin
            )
    return result.reshape(orbitals.shape)


def chebyshev_step(ext, pot_ref, c, p):
    here = ext[c, 4 + p]
    ny = here.shape[0]
    pot = pot_ref[:, p : p + 1, :]
    out = here * ((pot - (MIDDLE + 1.5 * STENCIL[0])) / SPREAD)
    for m in range(1, 5):
        beside = ext[c, 4 + p + m] + ext[c, 4 + p - m]
        beside = beside + jnp.concatenate([here[ny - m :], here[: ny - m]], axis=0)
        beside = beside + jnp.concatenate([here[m:], here[:m]], axis=0)
        beside = beside + pltpu.roll(here, m, 2) + pltpu.roll(here, here.shape[2] - m, 2)
        out = out + (-0.5 * STENCIL[m] / SPREAD) * beside
    return out


def inverse_factor(gram):
    size = gram.shape[0]
    lanes = lax.broadcasted_iota(jnp.int32, (ROWS, 2 * size), 1)
    rows = lax.broadcasted_iota(jnp.int32, (ROWS, 2 * size), 0)
    unit_rows = lax.broadcasted_iota(jnp.int32, (size, size), 0)
    unit_lanes = lax.broadcasted_iota(jnp.int32, (size, size), 1)
    unit = jnp.where(unit_rows == unit_lanes, 1.0, 0.0).astype(jnp.float32)
    whole = jnp.concatenate([gram, unit], axis=1)
    blocks = [whole[ROWS * k : ROWS * (k + 1)] for k in range(size // ROWS)]
    for j in range(size):
        own, at = divmod(j, ROWS)
        row = blocks[own][at : at + 1]
        row = row / row[:, j : j + 1]
        for k in range(own, size // ROWS):
            less = blocks[k] - blocks[k][:, j : j + 1] * row
            blocks[k] = jnp.where(rows > at, less, blocks[k]) if k == own else less
    scaled = []
    for k, block in enumerate(blocks):
        pivot = jnp.sum(jnp.where(lanes == rows + ROWS * k, block, 0.0), axis=1, keepdims=True)
        scaled.append(block[:, size:] / jnp.sqrt(pivot))
    return jnp.concatenate(scaled, axis=0)


def split(value):
    high = value.astype(jnp.bfloat16)
    return high, (value - high.astype(jnp.float32)).astype(jnp.bfloat16)


def kernel(
    n, x_ref, pot_ref, out_ref,
    ext, ext2, fil, fil0, both, near, far,
    send1, recv1, send2, recv2, sendx, recvx, sendn, recvn, sendf, recvf,
):
    chunks, planes, ny = x_ref.shape[:3]
    lines = planes * ny
    me = lax.axis_index("grid")
    band = lax.axis_index("band")
    right, left = lax.rem(me + 1, n), lax.rem(me + n - 1, n)
    inner = 4
    outer = n // inner
    q, zz = lax.rem(me, inner), lax.div(me, inner)
    near_peers = [zz * inner + lax.rem(q + k, inner) for k in range(1, inner)]
    far_peers = [lax.rem(zz + k, outer) * inner + q for k in range(1, outer)]
    partner = {"band": 1 - band}

    barrier = pltpu.get_barrier_semaphore()
    peers = [{"grid": d} for d in [left, right] + near_peers + far_peers] + [partner]
    for peer in peers:
        pl.semaphore_signal(barrier, inc=1, device_id=peer, device_id_type=MESH)
    pl.semaphore_wait(barrier, len(peers))

    own = pl.ds(4, planes)

    def halo(src, dst, send, recv, c, side):
        where = pl.ds(0, 4) if side == 0 else pl.ds(4 + planes, 4)
        return pltpu.make_async_remote_copy(
            src_ref=src, dst_ref=dst.at[c, where],
            send_sem=send.at[side, c], recv_sem=recv.at[side, c],
            device_id={"grid": right if side == 0 else left}, device_id_type=MESH,
        )

    def halo1(c, side):
        return halo(x_ref.at[c], ext, send1, recv1, c, side)

    def halo2(c, side):
        return halo(ext2.at[c, own], ext2, send2, recv2, c, side)

    def across(c, p):
        return pltpu.make_async_remote_copy(
            src_ref=fil.at[c, pl.ds(p * ny, ny)], dst_ref=fil0.at[c, pl.ds(p * ny, ny)],
            send_sem=sendx.at[c, p], recv_sem=recvx.at[c, p],
            device_id=partner, device_id_type=MESH,
        )

    def begin(c, carry):
        halo1(c, 0).start()
        halo1(c, 1).start()
        ext[c, own] = x_ref[c]
        return carry

    lax.fori_loop(0, chunks, begin, 0)

    def first(c, carry):
        halo1(c, 0).wait_recv()
        halo1(c, 1).wait_recv()
        for p in range(planes):
            ext2[c, 4 + p] = chebyshev_step(ext, pot_ref, c, p)
        halo2(c, 0).start()
        halo2(c, 1).start()
        return carry

    lax.fori_loop(0, chunks, first, 0)

    def second(c, carry):
        halo2(c, 0).wait_recv()
        halo2(c, 1).wait_recv()
        for p in range(planes):
            value = 2.0 * chebyshev_step(ext2, pot_ref, c, p) - ext[c, 4 + p]
            fil[c, pl.ds(p * ny, ny)] = value
            send_across(c, p)

        @pl.when(band == 0)
        def _():
            fil0[c] = fil[c]

        return carry

    def send_across(c, p):
        @pl.when(band == 0)
        def _():
            across(c, p).start()

    lax.fori_loop(0, chunks, second, 0)

    rows = chunks * ROWS
    size = 2 * rows

    def cast(ref, low_chunk, high_chunk, start):
        count = (high_chunk - low_chunk) * ROWS

        def one(i, carry):
            value = jnp.concatenate(
                [
                    ref[low_chunk:high_chunk, 2 * i + t].reshape(count, ref.shape[3])
                    for t in range(2)
                ],
                axis=1,
            )
            high, low = split(value)
            both[i, start : start + count] = high
            both[i, size + start : size + start + count] = low
            return carry

        lax.fori_loop(0, lines // 2, one, 0, unroll=4)

    def arrived(low_chunk, high_chunk):
        @pl.when(band == 1)
        def _():
            for c in range(low_chunk, high_chunk):
                for p in range(planes):
                    across(c, p).wait_recv()

    half_way = chunks // 2
    cast(fil, 0, chunks, rows)
    arrived(0, half_way)
    cast(fil0, 0, half_way, 0)
    arrived(half_way, chunks)
    cast(fil0, half_way, chunks, half_way * ROWS)

    def gram(i, total):
        tall = both[i]
        return total + lax.dot_general(
            tall, tall, (((1,), (1,)), ((), ())), preferred_element_type=jnp.float32
        )

    total = lax.fori_loop(
        0, lines // 2, gram, jnp.zeros((2 * size, 2 * size), jnp.float32), unroll=UNROLL
    )
    total = total[:size] + total[size:]
    total = total[:, :size] + total[:, size:]
    packed = jnp.concatenate([total[:rows], total[rows:]], axis=1)

    sent = []

    def exchange(value, slots, send, recv, place, peers, sources):
        slots[place] = value
        copies = [
            pltpu.make_async_remote_copy(
                src_ref=slots.at[place], dst_ref=slots.at[place],
                send_sem=send.at[k], recv_sem=recv.at[k],
                device_id={"grid": peer}, device_id_type=MESH,
            )
            for k, peer in enumerate(peers)
        ]
        for copy in copies:
            copy.start()
        for k, source in enumerate(sources):
            pltpu.make_async_remote_copy(
                src_ref=slots.at[source], dst_ref=slots.at[source],
                send_sem=send.at[k], recv_sem=recv.at[k],
                device_id={"grid": peers[k]}, device_id_type=MESH,
            ).wait_recv()
        sent.extend(copies)
        out = slots[0]
        for k in range(1, slots.shape[0]):
            out = out + slots[k]
        return out

    near_from = [lax.rem(q + inner - k, inner) for k in range(1, inner)]
    far_from = [lax.rem(zz + outer - k, outer) for k in range(1, outer)]
    packed = exchange(packed, near, sendn, recvn, q, near_peers, near_from)
    packed = exchange(packed, far, sendf, recvf, zz, far_peers, far_from)
    packed = packed / (lines * x_ref.shape[4] * n)
    inverse = inverse_factor(jnp.concatenate([packed[:, :size], packed[:, size:]], axis=0))
    weights = jnp.where(band == 0, inverse[:rows], inverse[rows:])
    high, low = split(weights)
    tall = jnp.concatenate([high, low], axis=0)
    wide = jnp.concatenate([tall, tall], axis=1)

    def final(i, carry):
        out = jnp.dot(wide, both[i], preferred_element_type=jnp.float32)
        out = out[:rows] + out[rows:]
        half = out.shape[1] // 2
        out_ref[2 * i] = out[:, :half]
        out_ref[2 * i + 1] = out[:, half:]
        return carry

    lax.fori_loop(0, lines // 2, final, 0, unroll=UNROLL)

    for copy in sent:
        copy.wait_send()
    for c in range(chunks):
        for side in range(2):
            halo1(c, side).wait_send()
            halo2(c, side).wait_send()

    @pl.when(band == 0)
    def _():
        for c in range(chunks):
            for p in range(planes):
                across(c, p).wait_send()


def on_device_two(n, orbitals, potential):
    rows, planes, ny, nz = orbitals.shape
    chunks = rows // ROWS
    x = orbitals.reshape(chunks, ROWS, planes, ny, nz).transpose(0, 2, 3, 1, 4)
    f32, dma = jnp.float32, pltpu.SemaphoreType.DMA
    out = pl.pallas_call(
        functools.partial(kernel, n),
        out_shape=jax.ShapeDtypeStruct((planes * ny, rows, nz), f32),
        in_specs=[pl.BlockSpec(memory_space=pltpu.VMEM)] * 2,
        out_specs=pl.BlockSpec(memory_space=pltpu.VMEM),
        scratch_shapes=[
            pltpu.VMEM((chunks, planes + 8, ny, ROWS, nz), f32),
            pltpu.VMEM((chunks, planes + 8, ny, ROWS, nz), f32),
            pltpu.VMEM((chunks, planes * ny, ROWS, nz), f32),
            pltpu.VMEM((chunks, planes * ny, ROWS, nz), f32),
            pltpu.VMEM((planes * ny // 2, 4 * rows, 2 * nz), jnp.bfloat16),
            pltpu.VMEM((4, rows, 4 * rows), f32),
            pltpu.VMEM((n // 4, rows, 4 * rows), f32),
            dma((2, chunks)), dma((2, chunks)), dma((2, chunks)), dma((2, chunks)),
            dma((chunks, planes)), dma((chunks, planes)),
            dma((3,)), dma((3,)), dma((n // 4 - 1,)), dma((n // 4 - 1,)),
        ],
        compiler_params=pltpu.CompilerParams(
            collective_id=0, has_side_effects=True, vmem_limit_bytes=40 * 1024 * 1024
        ),
    )(x, potential.transpose(1, 0, 2))
    return out.reshape(planes, ny, rows, nz).transpose(2, 0, 1, 3)


def solution(mesh):
    n = mesh.shape["grid"]
    one_kernel = mesh.shape["band"] == 2 and n % 4 == 0 and n > 4
    on_device = functools.partial(on_device_two, n) if one_kernel else on_device_any
    in_specs = (P("band", "grid", None, None), P("grid", None, None))
    out_specs = P("band", "grid", None, None)
    return jax.shard_map(
        on_device, mesh=mesh, in_specs=in_specs, out_specs=out_specs, check_vma=False
    )
```

```python
import functools

import jax
import jax.numpy as jnp
from jax import lax
from jax.experimental import pallas as pl
from jax.experimental.pallas import tpu as pltpu
from jax.sharding import PartitionSpec as P

STENCIL = (-205.0 / 72.0, 8.0 / 5.0, -1.0 / 5.0, 8.0 / 315.0, -1.0 / 560.0)
MIDDLE = 6.875
SPREAD = 3.875
ROWS = 8
UNROLL = 24
MESH = pl.DeviceIdType.MESH


def padded_2(cells, sides, width):
    for axis, dim in sides:
        count = lax.axis_size(axis)
        head = lax.slice_in_dim(cells, 0, width, axis=dim)
        tail = lax.slice_in_dim(cells, cells.shape[dim] - width, cells.shape[dim], axis=dim)
        cells = jnp.concatenate(
            [
                lax.ppermute(tail, axis, [(i, (i + 1) % count) for i in range(count)]),
                cells,
                lax.ppermute(head, axis, [((i + 1) % count, i) for i in range(count)]),
            ],
            axis=dim,
        )
    return cells


def from_root(value, axis, source):
    kept = jnp.where(lax.axis_index(axis) == source, value, 0).astype(value.dtype)
    return lax.psum(kept, axis)


def apply_ham(field, potential):
    padded = padded_2(field, (("grid", 1),), 4)
    planes = field.shape[1]
    laplace = 3.0 * STENCIL[0] * field
    for m in range(1, 5):
        beside_all = padded[:, 4 + m : 4 + m + planes] + padded[:, 4 - m : 4 - m + planes]
        beside_all = beside_all + jnp.roll(field, m, 2) + jnp.roll(field, -m, 2)
        beside_all = beside_all + jnp.roll(field, m, 3) + jnp.roll(field, -m, 3)
        laplace = laplace + STENCIL[m] * beside_all
    return -0.5 * laplace + potential[None] * field


def products(left, right):
    return jnp.dot(left, right.T, precision=lax.Precision.HIGHEST)


def on_device_any(orbitals, potential):
    first_step = (apply_ham(orbitals, potential) - MIDDLE * orbitals) / SPREAD
    second = 2.0 * (apply_ham(first_step, potential) - MIDDLE * first_step) / SPREAD - orbitals
    group_rows = orbitals.shape[0]
    filtered = second.reshape(group_rows, -1)
    total_cells = filtered.shape[1] * lax.axis_size("grid")
    position = lax.axis_index("band")
    groups = lax.axis_size("band")
    result = jnp.zeros_like(filtered)
    residual_block = filtered
    margin = lax.psum(products(filtered, filtered), "grid") / total_cells
    for h in range(groups):
        factor = jnp.linalg.cholesky(margin)
        orthonormal = lax.linalg.triangular_solve(
            factor, residual_block, left_side=True, lower=True
        )
        result = jnp.where(position == h, orthonormal, result)
        if h + 1 < groups:
            finished = from_root(orthonormal, "band", h)
            coeffs = lax.psum(products(finished, residual_block), "grid") / total_cells
            pending = position > h
            residual_block = jnp.where(
                pending,
                residual_block - jnp.dot(coeffs.T, finished, precision=lax.Precision.HIGHEST),
                residual_block,
            )
            margin = jnp.where(
                pending, margin - jnp.dot(coeffs.T, coeffs, precision=lax.Precision.HIGHEST), margin
            )
    return result.reshape(orbitals.shape)


def chebyshev_step(ext, pot_ref, c, p):
    here = ext[c, 4 + p]
    ny = here.shape[0]
    pot = pot_ref[:, p : p + 1, :]
    out = here * ((pot - (MIDDLE + 1.5 * STENCIL[0])) / SPREAD)
    for m in range(1, 5):
        beside = ext[c, 4 + p + m] + ext[c, 4 + p - m]
        beside = beside + jnp.concatenate([here[ny - m :], here[: ny - m]], axis=0)
        beside = beside + jnp.concatenate([here[m:], here[:m]], axis=0)
        beside = beside + pltpu.roll(here, m, 2) + pltpu.roll(here, here.shape[2] - m, 2)
        out = out + (-0.5 * STENCIL[m] / SPREAD) * beside
    return out


def inverse_factor(gram):
    size = gram.shape[0]
    lanes = lax.broadcasted_iota(jnp.int32, (ROWS, 2 * size), 1)
    rows = lax.broadcasted_iota(jnp.int32, (ROWS, 2 * size), 0)
    unit_rows = lax.broadcasted_iota(jnp.int32, (size, size), 0)
    unit_lanes = lax.broadcasted_iota(jnp.int32, (size, size), 1)
    unit = jnp.where(unit_rows == unit_lanes, 1.0, 0.0).astype(jnp.float32)
    whole = jnp.concatenate([gram, unit], axis=1)
    blocks = [whole[ROWS * k : ROWS * (k + 1)] for k in range(size // ROWS)]
    for j in range(size):
        own, at = divmod(j, ROWS)
        row = blocks[own][at : at + 1]
        row = row / row[:, j : j + 1]
        for k in range(own, size // ROWS):
            less = blocks[k] - blocks[k][:, j : j + 1] * row
            blocks[k] = jnp.where(rows > at, less, blocks[k]) if k == own else less
    scaled = []
    for k, block in enumerate(blocks):
        pivot = jnp.sum(jnp.where(lanes == rows + ROWS * k, block, 0.0), axis=1, keepdims=True)
        scaled.append(block[:, size:] / jnp.sqrt(pivot))
    return jnp.concatenate(scaled, axis=0)


def split(value):
    high = value.astype(jnp.bfloat16)
    return high, (value - high.astype(jnp.float32)).astype(jnp.bfloat16)


def kernel(
    n, x_ref, pot_ref, out_ref,
    ext, ext2, fil, fil0, both, near, far,
    send1, recv1, send2, recv2, sendx, recvx, sendn, recvn, sendf, recvf,
):
    chunks, planes, ny = x_ref.shape[:3]
    lines = planes * ny
    me = lax.axis_index("grid")
    band = lax.axis_index("band")
    right, left = lax.rem(me + 1, n), lax.rem(me + n - 1, n)
    inner = 4
    outer = n // inner
    q, zz = lax.rem(me, inner), lax.div(me, inner)
    near_peers = [zz * inner + lax.rem(q + k, inner) for k in range(1, inner)]
    far_peers = [lax.rem(zz + k, outer) * inner + q for k in range(1, outer)]
    partner = {"band": 1 - band}

    barrier = pltpu.get_barrier_semaphore()
    peers = [{"grid": d} for d in [left, right] + near_peers + far_peers] + [partner]
    for peer in peers:
        pl.semaphore_signal(barrier, inc=1, device_id=peer, device_id_type=MESH)
    pl.semaphore_wait(barrier, len(peers))

    own = pl.ds(4, planes)

    def halo(src, dst, send, recv, c, side):
        where = pl.ds(0, 4) if side == 0 else pl.ds(4 + planes, 4)
        return pltpu.make_async_remote_copy(
            src_ref=src, dst_ref=dst.at[c, where],
            send_sem=send.at[side, c], recv_sem=recv.at[side, c],
            device_id={"grid": right if side == 0 else left}, device_id_type=MESH,
        )

    def halo1(c, side):
        return halo(x_ref.at[c], ext, send1, recv1, c, side)

    def halo2(c, side):
        return halo(ext2.at[c, own], ext2, send2, recv2, c, side)

    def across(c, p):
        return pltpu.make_async_remote_copy(
            src_ref=fil.at[c, pl.ds(p * ny, ny)], dst_ref=fil0.at[c, pl.ds(p * ny, ny)],
            send_sem=sendx.at[c, p], recv_sem=recvx.at[c, p],
            device_id=partner, device_id_type=MESH,
        )

    def begin(c, carry):
        halo1(c, 0).start()
        halo1(c, 1).start()
        ext[c, own] = x_ref[c]
        return carry

    lax.fori_loop(0, chunks, begin, 0)

    def first(c, carry):
        halo1(c, 0).wait_recv()
        halo1(c, 1).wait_recv()
        for p in range(planes):
            ext2[c, 4 + p] = chebyshev_step(ext, pot_ref, c, p)
        halo2(c, 0).start()
        halo2(c, 1).start()
        return carry

    lax.fori_loop(0, chunks, first, 0)

    def second(c, carry):
        halo2(c, 0).wait_recv()
        halo2(c, 1).wait_recv()
        for p in range(planes):
            value = 2.0 * chebyshev_step(ext2, pot_ref, c, p) - ext[c, 4 + p]
            fil[c, pl.ds(p * ny, ny)] = value
            send_across(c, p)

        @pl.when(band == 0)
        def _():
            fil0[c] = fil[c]

        return carry

    def send_across(c, p):
        @pl.when(band == 0)
        def _():
            across(c, p).start()

    lax.fori_loop(0, chunks, second, 0)

    rows = chunks * ROWS
    size = 2 * rows

    def cast(ref, low_chunk, high_chunk, start):
        count = (high_chunk - low_chunk) * ROWS

        def one(i, carry):
            value = jnp.concatenate(
                [
                    ref[low_chunk:high_chunk, 2 * i + t].reshape(count, ref.shape[3])
                    for t in range(2)
                ],
                axis=1,
            )
            high, low = split(value)
            both[i, start : start + count] = high
            both[i, size + start : size + start + count] = low
            return carry

        lax.fori_loop(0, lines // 2, one, 0, unroll=12)

    def arrived(low_chunk, high_chunk):
        @pl.when(band == 1)
        def _():
            for c in range(low_chunk, high_chunk):
                for p in range(planes):
                    across(c, p).wait_recv()

    half_way = chunks // 2
    cast(fil, 0, chunks, rows)
    arrived(0, half_way)
    cast(fil0, 0, half_way, 0)
    arrived(half_way, chunks)
    cast(fil0, half_way, chunks, half_way * ROWS)

    def gram(i, total):
        tall = both[i]
        return total + lax.dot_general(
            tall, tall, (((1,), (1,)), ((), ())), preferred_element_type=jnp.float32
        )

    total = lax.fori_loop(
        0, lines // 2, gram, jnp.zeros((2 * size, 2 * size), jnp.float32), unroll=UNROLL
    )
    total = total[:size] + total[size:]
    total = total[:, :size] + total[:, size:]
    packed = jnp.concatenate([total[:rows], total[rows:]], axis=1)

    sent = []

    def exchange(value, slots, send, recv, place, peers, sources):
        slots[place] = value
        copies = [
            pltpu.make_async_remote_copy(
                src_ref=slots.at[place], dst_ref=slots.at[place],
                send_sem=send.at[k], recv_sem=recv.at[k],
                device_id={"grid": peer}, device_id_type=MESH,
            )
            for k, peer in enumerate(peers)
        ]
        for copy in copies:
            copy.start()
        for k, source in enumerate(sources):
            pltpu.make_async_remote_copy(
                src_ref=slots.at[source], dst_ref=slots.at[source],
                send_sem=send.at[k], recv_sem=recv.at[k],
                device_id={"grid": peers[k]}, device_id_type=MESH,
            ).wait_recv()
        sent.extend(copies)
        out = slots[0]
        for k in range(1, slots.shape[0]):
            out = out + slots[k]
        return out

    near_from = [lax.rem(q + inner - k, inner) for k in range(1, inner)]
    far_from = [lax.rem(zz + outer - k, outer) for k in range(1, outer)]
    packed = exchange(packed, near, sendn, recvn, q, near_peers, near_from)
    packed = exchange(packed, far, sendf, recvf, zz, far_peers, far_from)
    packed = packed / (lines * x_ref.shape[4] * n)
    inverse = inverse_factor(jnp.concatenate([packed[:, :size], packed[:, size:]], axis=0))
    weights = jnp.where(band == 0, inverse[:rows], inverse[rows:])
    high, low = split(weights)
    tall = jnp.concatenate([high, low], axis=0)
    wide = jnp.concatenate([tall, tall], axis=1)

    def final(i, carry):
        out = jnp.dot(wide, both[i], preferred_element_type=jnp.float32)
        out = out[:rows] + out[rows:]
        half = out.shape[1] // 2
        out_ref[2 * i] = out[:, :half]
        out_ref[2 * i + 1] = out[:, half:]
        return carry

    lax.fori_loop(0, lines // 2, final, 0, unroll=UNROLL)

    for copy in sent:
        copy.wait_send()
    for c in range(chunks):
        for side in range(2):
            halo1(c, side).wait_send()
            halo2(c, side).wait_send()

    @pl.when(band == 0)
    def _():
        for c in range(chunks):
            for p in range(planes):
                across(c, p).wait_send()


def on_device_two(n, orbitals, potential):
    rows, planes, ny, nz = orbitals.shape
    chunks = rows // ROWS
    x = orbitals.reshape(chunks, ROWS, planes, ny, nz).transpose(0, 2, 3, 1, 4)
    f32, dma = jnp.float32, pltpu.SemaphoreType.DMA
    out = pl.pallas_call(
        functools.partial(kernel, n),
        out_shape=jax.ShapeDtypeStruct((planes * ny, rows, nz), f32),
        in_specs=[pl.BlockSpec(memory_space=pltpu.VMEM)] * 2,
        out_specs=pl.BlockSpec(memory_space=pltpu.VMEM),
        scratch_shapes=[
            pltpu.VMEM((chunks, planes + 8, ny, ROWS, nz), f32),
            pltpu.VMEM((chunks, planes + 8, ny, ROWS, nz), f32),
            pltpu.VMEM((chunks, planes * ny, ROWS, nz), f32),
            pltpu.VMEM((chunks, planes * ny, ROWS, nz), f32),
            pltpu.VMEM((planes * ny // 2, 4 * rows, 2 * nz), jnp.bfloat16),
            pltpu.VMEM((4, rows, 4 * rows), f32),
            pltpu.VMEM((n // 4, rows, 4 * rows), f32),
            dma((2, chunks)), dma((2, chunks)), dma((2, chunks)), dma((2, chunks)),
            dma((chunks, planes)), dma((chunks, planes)),
            dma((3,)), dma((3,)), dma((n // 4 - 1,)), dma((n // 4 - 1,)),
        ],
        compiler_params=pltpu.CompilerParams(
            collective_id=0, has_side_effects=True, vmem_limit_bytes=40 * 1024 * 1024
        ),
    )(x, potential.transpose(1, 0, 2))
    return out.reshape(planes, ny, rows, nz).transpose(2, 0, 1, 3)


def solution(mesh):
    n = mesh.shape["grid"]
    one_kernel = mesh.shape["band"] == 2 and n % 4 == 0 and n > 4
    on_device = functools.partial(on_device_two, n) if one_kernel else on_device_any
    in_specs = (P("band", "grid", None, None), P("grid", None, None))
    out_specs = P("band", "grid", None, None)
    return jax.shard_map(
        on_device, mesh=mesh, in_specs=in_specs, out_specs=out_specs, check_vma=False
    )
```
